512 devices in a mesh: section: 32 (over z_lo, y), tensor: 16 (over x, z_hi, core).
Axes of the slice: x: 4, y: 4, z: 16 (z_hi: 2, z_lo: 8; z = z_hi * 8 + z_lo), core: 2. Of those that a mesh axis runs over, the one named last changes fastest.
Arguments:
- grad_codes: int32 [64, 256, 12288], P('section', None, 'tensor'), may hold values from -127 to 127
- token_scales: float32 [64, 256], P('section'), may hold values from 0.003 to 0.03
- loss_grads: bfloat16 [5, 256, 12288], P(None, None, 'tensor'), may hold values from -6 to 6
- entry_order: int32 [5], replicated, may hold values from 0 to 4, each once
- w_up: bfloat16 [64, 12288, 256], P('section', 'tensor'), may hold values from -0.375 to 0.375
- w_down: bfloat16 [64, 256, 12288], P('section', None, 'tensor'), may hold values from -0.0546875 to 0.0546875
- pre_act: bfloat16 [64, 5, 256, 256], P('section'), may hold values from -6 to 6
Outputs:
- held_grads: bfloat16 [64, 256, 12288], P('section', None, 'tensor')
- down_grad: bfloat16 [64, 256, 12288], P('section', None, 'tensor')
The draws below stay inside these ranges and needn't reach their ends.
Inputs may be any that keep to these rules, and one draw needn't show every extreme that they name: entry_order is a permutation of 0 .. 4.
All inputs are finite; a program needn't handle non-finite values.
Results may differ from the reference program's by a relative error of at most 0.015.
Values may be sent and summed in bfloat16 or wider, within the bound.
A program may use at most 64 MiB of HBM per device.

```python
import math
import jax
import jax.numpy as jnp

D = 12288
FF_BLOCK = 256
MBT = 256
TICKS = 5
SLOTS = 64
N_SECTION = 32


def set_ends(drawn, stream_key, smallest, largest):
    longest = drawn.shape.index(max(drawn.shape))
    spots = []
    for shift in (0, 1):
        where = [jax.random.randint(jax.random.fold_in(stream_key, axis), (), 0, length) for axis, length in enumerate(drawn.shape)]
        where[longest] = (where[longest] + shift) % drawn.shape[longest]
        spots.append(tuple(where))
    return drawn.at[spots[0]].set(smallest).at[spots[1]].set(largest)


def levels(rng, extent, pieces, smallest, high):
    factor_of = 1.0
    for axis_at, shards_of in pieces:
        steps = jax.random.uniform(jax.random.fold_in(jax.random.fold_in(rng, 6), axis_at), (shards_of,), jnp.float32, smallest / len(pieces), high / len(pieces))
        factor_of = factor_of * jnp.repeat(jnp.exp(steps), extent[axis_at] // shards_of).reshape((-1,) + (1,) * (len(extent) - 1 - axis_at))
    return factor_of


def normal_values(rng, dims, spread, bound, shards=(), held_as=jnp.bfloat16):
    drawn = jax.random.normal(rng, dims, jnp.float32) * spread
    if len(shards) > 0:
        drawn = levels(rng, dims, shards, -0.22, 0.18) * drawn
    return jnp.clip(drawn, min=-bound, max=bound).astype(held_as)


def setup_inputs(seed: int = 0) -> dict:
    arg_keys = jax.random.split(jax.random.key(seed), 8)
    grad_codes = set_ends(jax.random.randint(arg_keys[0], (SLOTS, MBT, D), -127, 128), jax.random.fold_in(arg_keys[0], 1), -127, 127).astype(jnp.int32)
    token_scales = jnp.clip(jnp.exp(math.log(0.03) - 2.3025851 * jax.random.uniform(arg_keys[1], (SLOTS, MBT), jnp.float32) ** levels(arg_keys[1], (SLOTS, MBT), ((0, 32),), -0.2, 0.2)), 0.003, 0.03)
    loss_grads = normal_values(arg_keys[2], (TICKS, MBT, D), 1.0, 6.0, ((2, 16),))
    entry_order = jax.random.permutation(arg_keys[3], TICKS).astype(jnp.int32)
    w_up = normal_values(arg_keys[4], (SLOTS, D, FF_BLOCK), FF_BLOCK ** -0.5, 0.375, ((0, 32), (1, 16)))
    w_down = normal_values(arg_keys[5], (SLOTS, FF_BLOCK, D), D ** -0.5, 0.0546875, ((0, 32), (2, 16)))
    pre_act = normal_values(arg_keys[6], (SLOTS, TICKS, MBT, FF_BLOCK), 1.0, 6.0, ((0, 32),))
    return dict(grad_codes=grad_codes, token_scales=token_scales, loss_grads=loss_grads, entry_order=entry_order, w_up=w_up, w_down=w_down, pre_act=pre_act)


def reference(grad_codes, token_scales, loss_grads, entry_order, w_up, w_down, pre_act):
    held_rows = (grad_codes.astype(jnp.float32) * token_scales[:, :, None]).astype(jnp.bfloat16)
    weight_grad = jnp.zeros((SLOTS, FF_BLOCK, D), jnp.float32)
    up_wide = w_up.astype(jnp.float32)
    down_wide = w_down.astype(jnp.float32)
    for tick_index in range(TICKS):
        held_wide = held_rows.astype(jnp.float32)
        hidden = jnp.einsum("smd,sfd->smf", held_wide, down_wide)
        masked = jnp.where(pre_act[:, tick_index] > 0, hidden, 0.0).astype(jnp.bfloat16)
        passed = (held_wide + jnp.einsum("smf,sdf->smd", masked.astype(jnp.float32), up_wide)).astype(jnp.bfloat16)
        active = jnp.maximum(pre_act[:, tick_index], 0).astype(jnp.float32)
        weight_grad = weight_grad + jnp.einsum("smf,smd->sfd", active, held_wide)
        sectioned = passed.reshape(N_SECTION, 2, MBT, D)
        entering = loss_grads[entry_order[tick_index]]
        group_low = jnp.concatenate([sectioned[1:, 0], sectioned[:1, 1]], axis=0)
        group_high = jnp.concatenate([sectioned[1:, 1], entering[None]], axis=0)
        held_rows = jnp.stack([group_low, group_high], axis=1).reshape(SLOTS, MBT, D)
    return held_rows, weight_grad.astype(jnp.bfloat16)
```

```python
import jax
import jax.numpy as jnp
from jax import lax
from jax.experimental import pallas as pl
from jax.experimental.pallas import tpu as pltpu
from jax.sharding import PartitionSpec as P

MESH = pl.DeviceIdType.MESH
F32 = jnp.float32
BF16 = jnp.bfloat16
HALVES = 2


def relay_kernel(dims, codes, scales, entry, w_up, w_down, pre_act, loss_hbm, held_out, grad_out,
                 loss_in, hbuf, passed, part, rs_in, zown, zsend, zin, masked, total, grad_vmem,
                 rs_send, rs_recv, z_send, z_recv, ag_send, ag_recv, h_send, h_recv, out_sem, loss_sem):
    sections, group, ticks, tokens, width = dims
    rows = tokens // HALVES
    piece = rows // group
    chains = 2 * HALVES
    steps = ticks * chains
    sec = lax.axis_index("section")
    ten = lax.axis_index("tensor")
    x_at = lax.div(ten, 4)
    z_at = lax.rem(lax.div(ten, 2), 2)
    core_at = lax.rem(ten, 2)
    mine = x_at * 2 + core_at

    def peer(rel):
        other = lax.rem(mine + rel, group)
        return other, (sec, lax.div(other, 2) * 4 + z_at * 2 + lax.rem(other, 2))

    z_partner = (sec, x_at * 4 + (1 - z_at) * 2 + core_at)
    below = (lax.rem(sec + sections - 1, sections), ten)
    above = (lax.rem(sec + 1, sections), ten)

    barrier = pltpu.get_barrier_semaphore()
    for rel in range(1, group):
        pl.semaphore_signal(barrier, inc=1, device_id=peer(rel)[1], device_id_type=MESH)
    for other in (z_partner, below, above):
        pl.semaphore_signal(barrier, inc=1, device_id=other, device_id_type=MESH)

    is_top = sec == sections - 1
    loss_copy = pltpu.make_async_copy(loss_hbm, loss_in, loss_sem)

    @pl.when(is_top)
    def _():
        loss_copy.start()

    total[...] = jnp.zeros_like(total)
    lanes = min(128, rows)
    for slot in range(2):
        for block in range(tokens // lanes):
            at = slice(block * lanes, (block + 1) * lanes)
            across = jnp.broadcast_to(scales[slot:slot + 1, at], (lanes, lanes)).T
            for col in range(width // lanes):
                cols = slice(col * lanes, (col + 1) * lanes)
                hbuf[0, slot, at, cols] = (codes[slot, at, cols].astype(F32) * across).astype(BF16)

    @pl.when(is_top)
    def _():
        loss_copy.wait()

    pl.semaphore_wait(barrier, group + 2)

    def where_of(step):
        tick = lax.div(step, chains)
        chain = lax.rem(step, chains)
        slot = 1 - lax.rem(chain, 2)
        half = lax.div(chain, 2)
        return tick, slot, half, pl.multiple_of(half * rows, rows)

    def h_copy(step):
        tick, slot, half, row = where_of(step)
        slot_to = slot * lax.div(sec + sections - 1, sections)
        return pltpu.make_async_remote_copy(
            src_ref=passed.at[step],
            dst_ref=hbuf.at[tick + 1, slot_to, pl.ds(row, rows)],
            send_sem=h_send.at[step],
            recv_sem=h_recv.at[tick, slot_to, half],
            device_id=below,
            device_id_type=MESH,
        )

    def arrive(tick, slot, half, row):
        enters = jnp.logical_and(is_top, slot == 1)

        @pl.when(jnp.logical_and(tick >= 1, jnp.logical_not(enters)))
        def _():
            here = hbuf.at[tick, slot, pl.ds(row, rows)]
            pltpu.make_async_copy(here, here, h_recv.at[tick - 1, slot, half]).wait()

        @pl.when(jnp.logical_and(tick >= 1, enters))
        def _():
            hbuf[tick, 1, pl.ds(row, rows), :] = loss_in[entry[lax.max(tick - 1, 0)], pl.ds(row, rows), :]

    def partial_sum(step):
        tick, slot, half, row = where_of(step)
        arrive(tick, slot, half, row)
        part[step] = lax.dot_general(
            hbuf[tick, slot, pl.ds(row, rows), :], w_down[slot], (((1,), (1,)), ((), ())),
            preferred_element_type=F32).astype(BF16)
        for rel in range(1, group):
            other, device = peer(rel)
            pltpu.make_async_remote_copy(
                src_ref=part.at[step, pl.ds(pl.multiple_of(other * piece, piece), piece)],
                dst_ref=rs_in.at[step, rel - 1],
                send_sem=rs_send.at[step],
                recv_sem=rs_recv.at[step],
                device_id=device,
                device_id_type=MESH,
            ).start()

    def wait_bytes(ref, sem):
        pltpu.make_async_copy(ref, ref, sem).wait()

    own_rows = pl.ds(pl.multiple_of(mine * piece, piece), piece)

    def reduce_group(step):
        wait_bytes(rs_in.at[step], rs_recv.at[step])
        acc = part[step, own_rows, :].astype(F32)
        for rel in range(1, group):
            acc = acc + rs_in[step, rel - 1].astype(F32)
        zown[step] = acc
        zsend[step] = acc.astype(BF16)
        z_copy(step).start()

    def z_copy(step):
        return pltpu.make_async_remote_copy(
            src_ref=zsend.at[step], dst_ref=zin.at[step], send_sem=z_send.at[step], recv_sem=z_recv.at[step],
            device_id=z_partner, device_id_type=MESH)

    def mask_and_gather(step):
        tick, slot, half, row = where_of(step)
        wait_bytes(zin.at[step], z_recv.at[step])
        hidden = zown[step] + zin[step].astype(F32)
        pre = pre_act[slot, tick, pl.ds(pl.multiple_of(row + mine * piece, piece), piece), :]
        masked[step, own_rows, :] = jnp.where(pre.astype(F32) > 0, hidden, 0.0).astype(BF16)
        for rel in range(1, group):
            _, device = peer(rel)
            pltpu.make_async_remote_copy(
                src_ref=masked.at[step, own_rows],
                dst_ref=masked.at[step, own_rows],
                send_sem=ag_send.at[step],
                recv_sem=ag_recv.at[step],
                device_id=device,
                device_id_type=MESH,
            ).start()

    def update(step):
        tick, slot, half, row = where_of(step)
        wait_bytes(rs_in.at[step], ag_recv.at[step])
        branch = lax.dot_general(
            masked[step], w_up[slot], (((1,), (1,)), ((), ())), preferred_element_type=F32)
        passed[step] = (hbuf[tick, slot, pl.ds(row, rows), :].astype(F32) + branch).astype(BF16)

        @pl.when(sec + slot > 0)
        def _():
            h_copy(step).start()

    def add_weight_grad(step):
        tick, slot, half, row = where_of(step)

        @pl.when(half == HALVES - 1)
        def _():
            active = jnp.maximum(pre_act[slot, tick], 0)
            total[slot] += lax.dot_general(
                active, hbuf[tick, slot], (((0,), (0,)), ((), ())), preferred_element_type=F32)

        @pl.when(jnp.logical_and(half == HALVES - 1, tick == ticks - 1))
        def _():
            grad_vmem[slot] = total[slot].astype(BF16)
            pltpu.make_async_copy(grad_vmem.at[slot], grad_out.at[slot], out_sem.at[slot]).start()

    def body(step, carry):
        @pl.when(step < steps)
        def _():
            partial_sum(step)

        @pl.when(step >= 1)
        def _():
            mask_and_gather(step - 1)

        @pl.when(step < steps)
        def _():
            reduce_group(step)

        @pl.when(step >= 1)
        def _():
            update(step - 1)
            add_weight_grad(step - 1)

        return carry

    lax.fori_loop(0, steps + 1, body, 0)

    for slot in (1, 0):
        for half in range(HALVES):
            row = half * rows
            arrive(ticks, slot, half, row)
        pltpu.make_async_copy(hbuf.at[ticks, slot], held_out.at[slot], out_sem.at[2 + slot]).start()

    def drain(step, carry):
        tick, slot, half, row = where_of(step)
        wait_bytes(rs_in.at[step], rs_send.at[step])
        wait_bytes(rs_in.at[step], ag_send.at[step])
        wait_bytes(zsend.at[step], z_send.at[step])

        @pl.when(sec + slot > 0)
        def _():
            wait_bytes(passed.at[step], h_send.at[step])

        return carry

    lax.fori_loop(0, steps, drain, 0)
    for slot in range(2):
        pltpu.make_async_copy(grad_vmem.at[slot], grad_out.at[slot], out_sem.at[slot]).wait()
        pltpu.make_async_copy(hbuf.at[ticks, slot], held_out.at[slot], out_sem.at[2 + slot]).wait()


def solution(mesh):
    sections, tensors = mesh.shape["section"], mesh.shape["tensor"]
    group = tensors // 2

    def per_device(grad_codes, token_scales, loss_grads, entry_order, w_up, w_down, pre_act):
        slots, tokens, width = grad_codes.shape
        ticks, hid = pre_act.shape[1], pre_act.shape[3]
        rows = tokens // HALVES
        piece = rows // group
        steps = ticks * slots * HALVES
        vmem = pl.BlockSpec(memory_space=pltpu.VMEM)
        hbm = pl.BlockSpec(memory_space=pl.ANY)
        dma = pltpu.SemaphoreType.DMA
        out = jax.ShapeDtypeStruct((slots, tokens, width), BF16)
        return pl.pallas_call(
            lambda *refs: relay_kernel((sections, group, ticks, tokens, width), *refs),
            out_shape=(out, jax.ShapeDtypeStruct((slots, hid, width), BF16)),
            in_specs=[vmem, vmem, pl.BlockSpec(memory_space=pltpu.SMEM), vmem, vmem, vmem, hbm],
            out_specs=(hbm, hbm),
            scratch_shapes=[
                pltpu.VMEM((ticks, tokens, width), BF16),
                pltpu.VMEM((ticks + 1, slots, tokens, width), BF16),
                pltpu.VMEM((steps, rows, width), BF16),
                pltpu.VMEM((steps, rows, hid), BF16),
                pltpu.VMEM((steps, group - 1, piece, hid), BF16),
                pltpu.VMEM((steps, piece, hid), F32),
                pltpu.VMEM((steps, piece, hid), BF16),
                pltpu.VMEM((steps, piece, hid), BF16),
                pltpu.VMEM((steps, rows, hid), BF16),
                pltpu.VMEM((slots, hid, width), F32),
                pltpu.VMEM((slots, hid, width), BF16),
                dma((steps,)), dma((steps,)), dma((steps,)), dma((steps,)),
                dma((steps,)), dma((steps,)), dma((steps,)), dma((ticks, slots, HALVES)),
                dma((4,)), dma,
            ],
            compiler_params=pltpu.CompilerParams(
                collective_id=0, has_side_effects=True, vmem_limit_bytes=48 * 1024 * 1024),
            cost_estimate=pl.CostEstimate(flops=3 * 10**9, bytes_accessed=8 * 10**6, transcendentals=0),
        )(grad_codes, token_scales, entry_order, w_up, w_down, pre_act, loss_grads)

    placed = (
        P("section", None, "tensor"),
        P("section", None),
        P(None, None, "tensor"),
        P(),
        P("section", "tensor", None),
        P("section", None, "tensor"),
        P("section", None, None, None),
    )
    return jax.shard_map(
        per_device,
        mesh=mesh,
        in_specs=placed,
        out_specs=(P("section", None, "tensor"), P("section", None, "tensor")),
        check_vma=False,
    )
```

```python
import jax
import jax.numpy as jnp
from jax import lax
from jax.experimental import pallas as pl
from jax.experimental.pallas import tpu as pltpu
from jax.sharding import PartitionSpec as P

MESH = pl.DeviceIdType.MESH
F32 = jnp.float32
BF16 = jnp.bfloat16
CHAINS = 4
NT = (((1,), (1,)), ((), ()))
TN = (((0,), (0,)), ((), ()))


def relay_kernel(dims, scales, entry, codes_hbm, up_hbm, down_hbm, pre_hbm, loss_hbm, held_out, grad_out,
                 codes, w_up, w_down, pre_act, loss_in, down_in, hbuf, passed, part, rs_in, gsum, msg, masked,
                 cross, total, grad_vmem, load_sem, rs_send, rs_recv, msg_send, msg_recv, ag_send, ag_recv,
                 g_send, g_recv, h_send, h_recv, down_send, down_recv, held_sem, grad_sem):
    sections, group, ticks, tokens, width = dims
    rows = tokens // 2
    piece = rows // group
    first_q, first_g, first_top = CHAINS, CHAINS * ticks, CHAINS * (ticks + 1)
    jobs_q = CHAINS * (ticks - 1)
    steps = CHAINS * ticks
    sec = lax.axis_index("section")
    ten = lax.axis_index("tensor")
    x_at = lax.div(ten, 4)
    z_at = lax.rem(lax.div(ten, 2), 2)
    core_at = lax.rem(ten, 2)
    mine = x_at * 2 + core_at
    partner = x_at * 4 + (1 - z_at) * 2 + core_at
    sec_below = lax.rem(sec + sections - 1, sections)
    sec_above = lax.rem(sec + 1, sections)
    is_top = sec == sections - 1
    keeps = lax.div(sec + sections - 1, sections)
    own_rows = pl.ds(pl.multiple_of(mine * piece, piece), piece)

    def peer(rel):
        other = lax.rem(mine + rel, group)
        return other, (sec, lax.div(other, 2) * 4 + z_at * 2 + lax.rem(other, 2))

    def send(src, dst, ssem, rsem, device):
        return pltpu.make_async_remote_copy(
            src_ref=src, dst_ref=dst, send_sem=ssem, recv_sem=rsem, device_id=device, device_id_type=MESH)

    def wait_bytes(ref, sem):
        pltpu.make_async_copy(ref, ref, sem).wait()

    barrier = pltpu.get_barrier_semaphore()
    greeted = [peer(rel)[1] for rel in range(1, group)]
    greeted += [(sec, partner), (sec_below, ten), (sec_above, ten), (sec_below, partner), (sec_above, partner)]
    for other in greeted:
        pl.semaphore_signal(barrier, inc=1, device_id=other, device_id_type=MESH)

    loads = [pltpu.make_async_copy(src, dst, load_sem.at[i]) for i, (src, dst) in enumerate((
        (codes_hbm, codes), (down_hbm, w_down), (up_hbm, w_up), (pre_hbm, pre_act), (loss_hbm, loss_in)))]
    for load in loads[:4]:
        load.start()

    @pl.when(is_top)
    def _():
        loads[4].start()

    total[...] = jnp.zeros_like(total)
    loads[0].wait()
    lanes = min(128, rows)
    for slot in range(2):
        for block in range(tokens // lanes):
            at = slice(block * lanes, (block + 1) * lanes)
            across = jnp.broadcast_to(scales[slot:slot + 1, at], (lanes, lanes)).T
            for col in range(width // lanes):
                cols = slice(col * lanes, (col + 1) * lanes)
                hbuf[0, slot, at, cols] = (codes[slot, at, cols].astype(F32) * across).astype(BF16)
    loads[1].wait()
    pl.semaphore_wait(barrier, len(greeted))

    def down_copy(slot, slot_to):
        return send(w_down.at[slot], down_in.at[slot_to], down_send.at[slot], down_recv.at[slot_to], (sec_above, ten))

    @pl.when(is_top)
    def _():
        down_copy(0, 1).start()

    @pl.when(jnp.logical_not(is_top))
    def _():
        down_copy(1, 1).start()
        down_copy(0, 0).start()

    def where_of(step):
        tick = lax.div(step, CHAINS)
        chain = lax.rem(step, CHAINS)
        half = lax.rem(chain, 2)
        return tick, 1 - lax.div(chain, 2), half, pl.multiple_of(half * rows, rows)

    def goes_down(slot):
        return sec + slot > 0

    def enters(slot):
        return sec + slot == sections

    def scatter(job):
        for rel in range(1, group):
            other, device = peer(rel)
            send(part.at[job, pl.ds(pl.multiple_of(other * piece, piece), piece)], rs_in.at[job, rel - 1],
                 rs_send.at[job], rs_recv.at[job], device).start()

    def gathered(job):
        wait_bytes(rs_in.at[job], rs_recv.at[job])
        acc = part[job, own_rows, :].astype(F32)
        for rel in range(1, group):
            acc = acc + rs_in[job, rel - 1].astype(F32)
        return acc

    def own_partial(tick, slot, row, job):
        part[job] = lax.dot_general(
            hbuf[tick, slot, pl.ds(row, rows), :], w_down[slot], NT, preferred_element_type=F32).astype(BF16)
        scatter(job)

    def own_exchange(tick, slot, half, job):
        gsum[job] = gathered(job).astype(BF16)
        msg[tick, slot, half, z_at] = gsum[job]
        send(gsum.at[job], msg.at[tick, slot, half, z_at], msg_send.at[job], msg_recv.at[tick, slot, half],
             (sec, partner)).start()

    def arrive(tick, slot, half, row):
        @pl.when(jnp.logical_not(enters(slot)))
        def _():
            wait_bytes(hbuf.at[tick, slot, pl.ds(row, rows)], h_recv.at[tick - 1, slot, half])

    def look_ahead(step):
        tick, slot, half, row = where_of(step)

        @pl.when(jnp.logical_and(step < jobs_q, goes_down(slot)))
        def _():
            job = first_q + step
            part[job] = lax.dot_general(
                hbuf[tick, slot, pl.ds(row, rows), :], down_in[slot], NT, preferred_element_type=F32).astype(BF16)
            scatter(job)

    def pass_sum(step):
        tick, slot, half, row = where_of(step)

        @pl.when(jnp.logical_and(step < jobs_q, goes_down(slot)))
        def _():
            job = first_q + step
            gsum[job] = (gathered(job) + jnp.dot(
                masked[step, own_rows, :], cross[slot], preferred_element_type=F32)).astype(BF16)
            for to in (ten, partner):
                send(gsum.at[job], msg.at[tick + 1, slot * keeps, half, z_at], msg_send.at[job],
                     msg_recv.at[tick + 1, slot * keeps, half], (sec_below, to)).start()

    def finish_hidden(step):
        tick, slot, half, row = where_of(step)
        from_own = jnp.logical_or(tick == 0, enters(slot))

        @pl.when(from_own)
        def _():
            wait_bytes(gsum.at[0], msg_recv.at[tick, slot, half])

        @pl.when(jnp.logical_not(from_own))
        def _():
            wait_bytes(msg.at[tick, slot, half], msg_recv.at[tick, slot, half])

        hidden = msg[tick, slot, half, 0].astype(F32) + msg[tick, slot, half, 1].astype(F32)
        pre = pre_act[slot, tick, pl.ds(pl.multiple_of(row + mine * piece, piece), piece), :]
        masked[step, own_rows, :] = jnp.where(pre.astype(F32) > 0, hidden, 0.0).astype(BF16)
        for rel in range(1, group):
            send(masked.at[step, own_rows], masked.at[step, own_rows], ag_send.at[step], ag_recv.at[step],
                 peer(rel)[1]).start()

    def update(step):
        tick, slot, half, row = where_of(step)
        wait_bytes(rs_in.at[0], ag_recv.at[step])

        @pl.when(goes_down(slot))
        def _():
            branch = lax.dot_general(masked[step], w_up[slot], NT, preferred_element_type=F32)
            passed[step] = (hbuf[tick, slot, pl.ds(row, rows), :].astype(F32) + branch).astype(BF16)
            send(passed.at[step], hbuf.at[tick + 1, slot * keeps, pl.ds(row, rows)], h_send.at[step],
                 h_recv.at[tick, slot * keeps, half], (sec_below, ten)).start()

    def add_weight_grad(step):
        tick, slot, half, row = where_of(step)

        @pl.when(half == 1)
        def _():
            active = jnp.maximum(pre_act[slot, tick], 0)
            total[slot] += lax.dot_general(active, hbuf[tick, slot], TN, preferred_element_type=F32)

        @pl.when(jnp.logical_and(half == 1, tick == ticks - 1))
        def _():
            grad_vmem[slot] = total[slot].astype(BF16)
            pltpu.make_async_copy(grad_vmem.at[slot], grad_out.at[slot], grad_sem.at[slot]).start()

    def cross_scatter(slot):
        @pl.when(goes_down(slot))
        def _():
            wait_bytes(down_in.at[slot], down_recv.at[slot])
            term = lax.dot_general(w_up[slot], down_in[slot], (((0,), (1,)), ((), ())), preferred_element_type=F32)
            for half in range(2):
                part[first_g + slot * 2 + half] = term[half * rows:(half + 1) * rows].astype(BF16)
                scatter(first_g + slot * 2 + half)

    def cross_gather(slot):
        @pl.when(goes_down(slot))
        def _():
            for half in range(2):
                job = first_g + slot * 2 + half
                at = pl.ds(pl.multiple_of(half * rows + mine * piece, piece), piece)
                cross[slot, at, :] = gathered(job).astype(BF16)
                for rel in range(1, group):
                    send(cross.at[slot, at], cross.at[slot, at], g_send.at[slot * 2 + half],
                         g_recv.at[slot * 2 + half], peer(rel)[1]).start()

    def cross_wait(slot):
        @pl.when(goes_down(slot))
        def _():
            for half in range(2):
                wait_bytes(rs_in.at[0], g_recv.at[slot * 2 + half])

    def each(first, last, do):
        def body(step, carry):
            do(step)
            return carry

        lax.fori_loop(first, last, body, 0)

    def start_own(step):
        tick, slot, half, row = where_of(step)
        own_partial(0, slot, row, step)

    def exchange_own(step):
        tick, slot, half, row = where_of(step)
        own_exchange(0, slot, half, step)

    each(0, CHAINS, start_own)
    loads[2].wait()
    loads[3].wait()
    each(0, CHAINS, exchange_own)

    @pl.when(is_top)
    def _():
        loads[4].wait()
        for tick in range(1, ticks + 1):
            hbuf[tick, 1] = loss_in[entry[tick - 1]]

        def start_top(job):
            half = lax.rem(job, 2)
            own_partial(1 + lax.div(job, 2), 1, pl.multiple_of(half * rows, rows), first_top + job)

        def exchange_top(job):
            own_exchange(1 + lax.div(job, 2), 1, lax.rem(job, 2), first_top + job)

        each(0, 2 * (ticks - 1), start_top)
        each(0, 2 * (ticks - 1), exchange_top)

    cross_scatter(1)
    each(0, 2, look_ahead)
    each(0, CHAINS, finish_hidden)
    cross_gather(1)
    each(0, CHAINS, update)
    cross_scatter(0)
    each(2, CHAINS, look_ahead)
    cross_wait(1)
    each(0, 2, pass_sum)
    each(0, CHAINS, add_weight_grad)
    cross_gather(0)

    def take(step):
        tick, slot, half, row = where_of(step)
        arrive(tick, slot, half, row)
        look_ahead(step)

    take(CHAINS)
    cross_wait(0)
    pass_sum(2)
    finish_hidden(CHAINS)

    def main(step):
        pass_sum(step - 1)

        @pl.when(step + 1 < steps)
        def _():
            finish_hidden(step + 1)

        update(step)

        @pl.when(step + 1 < steps)
        def _():
            take(step + 1)
            add_weight_grad(step + 1)

    each(CHAINS, steps, main)

    def held_copy(chain):
        tick, slot, half, row = where_of(chain)
        return pltpu.make_async_copy(
            hbuf.at[ticks, slot, pl.ds(row, rows)], held_out.at[slot, pl.ds(row, rows)], held_sem.at[chain])

    def hand_out(chain):
        tick, slot, half, row = where_of(chain)
        arrive(ticks, slot, half, row)
        held_copy(chain).start()

    each(0, CHAINS, hand_out)

    def drain(step):
        tick, slot, half, row = where_of(step)
        wait_bytes(rs_in.at[0], ag_send.at[step])

        @pl.when(goes_down(slot))
        def _():
            wait_bytes(passed.at[step], h_send.at[step])

        @pl.when(jnp.logical_and(step < jobs_q, goes_down(slot)))
        def _():
            wait_bytes(rs_in.at[0], rs_send.at[first_q + step])
            wait_bytes(msg.at[0, 0, 0], msg_send.at[first_q + step])

    def drain_own(job):
        wait_bytes(rs_in.at[0], rs_send.at[job])
        wait_bytes(gsum.at[0], msg_send.at[job])

    def drain_cross(job):
        @pl.when(goes_down(lax.div(job, 2)))
        def _():
            wait_bytes(rs_in.at[0], rs_send.at[first_g + job])
            wait_bytes(rs_in.at[0], g_send.at[job])

    each(0, steps, drain)
    each(0, CHAINS, drain_own)
    each(0, CHAINS, drain_cross)
    wait_bytes(w_down.at[0], down_send.at[0])

    @pl.when(is_top)
    def _():
        each(first_top, first_top + 2 * (ticks - 1), drain_own)

    @pl.when(jnp.logical_not(is_top))
    def _():
        wait_bytes(w_down.at[1], down_send.at[1])

    for slot in range(2):
        pltpu.make_async_copy(grad_vmem.at[slot], grad_out.at[slot], grad_sem.at[slot]).wait()
    for chain in range(CHAINS):
        held_copy(chain).wait()


def solution(mesh):
    sections, tensors = mesh.shape["section"], mesh.shape["tensor"]
    group = tensors // 2

    def per_device(grad_codes, token_scales, loss_grads, entry_order, w_up, w_down, pre_act):
        slots, tokens, width = grad_codes.shape
        ticks, hid = pre_act.shape[1], pre_act.shape[3]
        rows = tokens // 2
        piece = rows // group
        steps = ticks * CHAINS
        jobs = CHAINS * (ticks + 1) + 2 * (ticks - 1)
        vmem = pl.BlockSpec(memory_space=pltpu.VMEM)
        hbm = pl.BlockSpec(memory_space=pl.ANY)
        dma = pltpu.SemaphoreType.DMA
        return pl.pallas_call(
            lambda *refs: relay_kernel((sections, group, ticks, tokens, width), *refs),
            out_shape=(jax.ShapeDtypeStruct((slots, tokens, width), BF16),
                       jax.ShapeDtypeStruct((slots, hid, width), BF16)),
            in_specs=[vmem, pl.BlockSpec(memory_space=pltpu.SMEM), hbm, hbm, hbm, hbm, hbm],
            out_specs=(hbm, hbm),
            scratch_shapes=[
                pltpu.VMEM((slots, tokens, width), jnp.int32),
                pltpu.VMEM((slots, width, hid), BF16),
                pltpu.VMEM((slots, hid, width), BF16),
                pltpu.VMEM((slots, ticks, tokens, hid), BF16),
                pltpu.VMEM((ticks, tokens, width), BF16),
                pltpu.VMEM((slots, hid, width), BF16),
                pltpu.VMEM((ticks + 1, slots, tokens, width), BF16),
                pltpu.VMEM((steps, rows, width), BF16),
                pltpu.VMEM((jobs, rows, hid), BF16),
                pltpu.VMEM((jobs, group - 1, piece, hid), BF16),
                pltpu.VMEM((jobs, piece, hid), BF16),
                pltpu.VMEM((ticks, slots, 2, 2, piece, hid), BF16),
                pltpu.VMEM((steps, rows, hid), BF16),
                pltpu.VMEM((slots, hid, hid), BF16),
                pltpu.VMEM((slots, hid, width), F32),
                pltpu.VMEM((slots, hid, width), BF16),
                dma((5,)), dma((jobs,)), dma((jobs,)), dma((jobs,)), dma((ticks, slots, 2)), dma((steps,)),
                dma((steps,)), dma((CHAINS,)), dma((CHAINS,)), dma((steps,)), dma((ticks, slots, 2)),
                dma((slots,)), dma((slots,)), dma((CHAINS,)), dma((slots,)),
            ],
            compiler_params=pltpu.CompilerParams(
                collective_id=0, has_side_effects=True, vmem_limit_bytes=56 * 1024 * 1024),
            cost_estimate=pl.CostEstimate(flops=4 * 10**9, bytes_accessed=9 * 10**6, transcendentals=0),
        )(token_scales, entry_order, grad_codes, w_up, w_down, pre_act, loss_grads)

    placed = (
        P("section", None, "tensor"),
        P("section", None),
        P(None, None, "tensor"),
        P(),
        P("section", "tensor", None),
        P("section", None, "tensor"),
        P("section", None, None, None),
    )
    return jax.shard_map(
        per_device,
        mesh=mesh,
        in_specs=placed,
        out_specs=(P("section", None, "tensor"), P("section", None, "tensor")),
        check_vma=False,
    )
```

```python
import jax
import jax.numpy as jnp
from jax import lax
from jax.experimental import pallas as pl
from jax.experimental.pallas import tpu as pltpu
from jax.sharding import PartitionSpec as P

MESH = pl.DeviceIdType.MESH
F32 = jnp.float32
BF16 = jnp.bfloat16
CHAINS = 4
NT = (((1,), (1,)), ((), ()))
TN = (((0,), (0,)), ((), ()))


def relay_kernel(dims, scales, entry, codes_hbm, up_hbm, down_hbm, pre_hbm, loss_hbm, held_out, grad_out,
                 codes, w_up, w_down, pre_act, loss_in, down_in, hbuf, passed, part, rs_in, gsum, msg, masked,
                 cross, total, load_sem, rs_send, rs_recv, msg_send, msg_recv, ag_send, ag_recv,
                 g_send, g_recv, h_send, h_recv, down_send, down_recv):
    sections, group, ticks, tokens, width = dims
    rows = tokens // 2
    piece = rows // group
    first_q, first_g, first_top = CHAINS, CHAINS * ticks, CHAINS * (ticks + 1)
    jobs_q = CHAINS * (ticks - 1)
    steps = CHAINS * ticks
    sec = lax.axis_index("section")
    ten = lax.axis_index("tensor")
    x_at = lax.div(ten, 4)
    z_at = lax.rem(lax.div(ten, 2), 2)
    core_at = lax.rem(ten, 2)
    mine = x_at * 2 + core_at
    partner = x_at * 4 + (1 - z_at) * 2 + core_at
    sec_below = lax.rem(sec + sections - 1, sections)
    sec_above = lax.rem(sec + 1, sections)
    is_top = sec == sections - 1
    keeps = lax.div(sec + sections - 1, sections)
    own_rows = pl.ds(pl.multiple_of(mine * piece, piece), piece)

    def peer(rel):
        other = lax.rem(mine + rel, group)
        return other, (sec, lax.div(other, 2) * 4 + z_at * 2 + lax.rem(other, 2))

    def send(src, dst, ssem, rsem, device):
        return pltpu.make_async_remote_copy(
            src_ref=src, dst_ref=dst, send_sem=ssem, recv_sem=rsem, device_id=device, device_id_type=MESH)

    def wait_bytes(ref, sem):
        pltpu.make_async_copy(ref, ref, sem).wait()

    def down_copy(slot, slot_to):
        return send(w_down.at[slot], down_in.at[slot_to], down_send.at[slot], down_recv.at[slot_to], (sec_above, ten))

    def where_of(step):
        tick = lax.div(step, CHAINS)
        chain = lax.rem(step, CHAINS)
        half = lax.rem(chain, 2)
        return tick, 1 - lax.div(chain, 2), half, pl.multiple_of(half * rows, rows)

    def goes_down(slot):
        return sec + slot > 0

    def enters(slot):
        return sec + slot == sections

    def scatter(job):
        for rel in range(1, group):
            other, device = peer(rel)
            send(part.at[job, pl.ds(pl.multiple_of(other * piece, piece), piece)], rs_in.at[job, rel - 1],
                 rs_send.at[job], rs_recv.at[job], device).start()

    def gathered(job):
        wait_bytes(rs_in.at[job], rs_recv.at[job])
        acc = part[job, own_rows, :].astype(F32)
        for rel in range(1, group):
            acc = acc + rs_in[job, rel - 1].astype(F32)
        return acc

    def own_partial(tick, slot, row, job):
        part[job] = lax.dot_general(
            hbuf[tick, slot, pl.ds(row, rows), :], w_down[slot], NT, preferred_element_type=F32).astype(BF16)
        scatter(job)

    def own_exchange(tick, slot, half, job):
        gsum[job] = gathered(job).astype(BF16)
        msg[tick, slot, half, z_at] = gsum[job]
        send(gsum.at[job], msg.at[tick, slot, half, z_at], msg_send.at[job], msg_recv.at[tick, slot, half],
             (sec, partner)).start()

    def arrive(tick, slot, half, row):
        @pl.when(jnp.logical_not(enters(slot)))
        def _():
            wait_bytes(hbuf.at[tick, slot, pl.ds(row, rows)], h_recv.at[tick - 1, slot, half])

    def look_ahead(step):
        tick, slot, half, row = where_of(step)

        @pl.when(jnp.logical_and(step < jobs_q, goes_down(slot)))
        def _():
            job = first_q + step
            part[job] = lax.dot_general(
                hbuf[tick, slot, pl.ds(row, rows), :], down_in[slot], NT, preferred_element_type=F32).astype(BF16)
            scatter(job)

    def send_sum(step):
        tick, slot, half, row = where_of(step)
        for to in (ten, partner):
            send(gsum.at[first_q + step], msg.at[tick + 1, slot * keeps, half, z_at], msg_send.at[first_q + step],
                 msg_recv.at[tick + 1, slot * keeps, half], (sec_below, to)).start()

    def pass_sum(step):
        tick, slot, half, row = where_of(step)

        @pl.when(jnp.logical_and(step < jobs_q, goes_down(slot)))
        def _():
            @pl.when(jnp.logical_and(tick == 1, half == 0))
            def _():
                for part_of in range(2):
                    wait_bytes(rs_in.at[0], g_recv.at[slot * 2 + part_of])

            gsum[first_q + step] = (gathered(first_q + step) + jnp.dot(
                masked[step, own_rows, :], cross[slot], preferred_element_type=F32)).astype(BF16)
            send_sum(step)

    def finish_hidden(step):
        tick, slot, half, row = where_of(step)
        from_own = jnp.logical_or(tick == 0, enters(slot))

        @pl.when(from_own)
        def _():
            wait_bytes(gsum.at[0], msg_recv.at[tick, slot, half])

        @pl.when(jnp.logical_not(from_own))
        def _():
            wait_bytes(msg.at[tick, slot, half], msg_recv.at[tick, slot, half])

        hidden = msg[tick, slot, half, 0].astype(F32) + msg[tick, slot, half, 1].astype(F32)
        pre = pre_act[slot, tick, pl.ds(pl.multiple_of(row + mine * piece, piece), piece), :]
        masked[step, own_rows, :] = jnp.where(pre.astype(F32) > 0, hidden, 0.0).astype(BF16)
        for rel in range(1, group):
            send(masked.at[step, own_rows], masked.at[step, own_rows], ag_send.at[step], ag_recv.at[step],
                 peer(rel)[1]).start()

    def update(step):
        tick, slot, half, row = where_of(step)
        wait_bytes(rs_in.at[0], ag_recv.at[step])

        @pl.when(goes_down(slot))
        def _():
            branch = lax.dot_general(masked[step], w_up[slot], NT, preferred_element_type=F32)
            passed[step] = (hbuf[tick, slot, pl.ds(row, rows), :].astype(F32) + branch).astype(BF16)
            send(passed.at[step], hbuf.at[tick + 1, slot * keeps, pl.ds(row, rows)], h_send.at[step],
                 h_recv.at[tick, slot * keeps, half], (sec_below, ten)).start()

    def add_weight_grad(step):
        tick, slot, half, row = where_of(step)

        @pl.when(half == 1)
        def _():
            active = jnp.maximum(pre_act[slot, tick], 0)
            total[slot] += lax.dot_general(active, hbuf[tick, slot], TN, preferred_element_type=F32)

        @pl.when(jnp.logical_and(half == 1, tick == ticks - 1))
        def _():
            grad_out[slot] = total[slot].astype(BF16)

    def down_wait(slot):
        @pl.when(goes_down(slot))
        def _():
            wait_bytes(down_in.at[slot], down_recv.at[slot])

    def cross_scatter(slot):
        @pl.when(goes_down(slot))
        def _():
            term = lax.dot_general(w_up[slot], down_in[slot], (((0,), (1,)), ((), ())), preferred_element_type=F32)
            for half in range(2):
                part[first_g + slot * 2 + half] = term[half * rows:(half + 1) * rows].astype(BF16)
                scatter(first_g + slot * 2 + half)

    def cross_gather(slot):
        @pl.when(goes_down(slot))
        def _():
            for half in range(2):
                job = first_g + slot * 2 + half
                at = pl.ds(pl.multiple_of(half * rows + mine * piece, piece), piece)
                cross[slot, at, :] = gathered(job).astype(BF16)
                for rel in range(1, group):
                    send(cross.at[slot, at], cross.at[slot, at], g_send.at[slot * 2 + half],
                         g_recv.at[slot * 2 + half], peer(rel)[1]).start()

    def each(first, last, do):
        def body(step, carry):
            do(step)
            return carry

        lax.fori_loop(first, last, body, 0)

    def exchange_own(step):
        tick, slot, half, row = where_of(step)
        own_exchange(0, slot, half, step)

    def first_product(step):
        tick, slot, half, row = where_of(step)
        part[step] = lax.dot_general(
            hbuf[0, slot, pl.ds(row, rows), :], w_down[slot], NT, preferred_element_type=F32).astype(BF16)

    barrier = pltpu.get_barrier_semaphore()
    greeted = [peer(rel)[1] for rel in range(1, group)]
    greeted += [(sec, partner), (sec_below, ten), (sec_above, ten), (sec_below, partner), (sec_above, partner)]
    for other in greeted:
        pl.semaphore_signal(barrier, inc=1, device_id=other, device_id_type=MESH)

    loads = [pltpu.make_async_copy(src, dst, load_sem.at[i]) for i, (src, dst) in enumerate((
        (codes_hbm, codes), (down_hbm, w_down), (up_hbm, w_up), (pre_hbm, pre_act), (loss_hbm, loss_in)))]
    for load in loads[:4]:
        load.start()

    @pl.when(is_top)
    def _():
        loads[4].start()

    total[...] = jnp.zeros_like(total)
    loads[0].wait()
    lanes = min(128, rows)
    for slot in range(2):
        for block in range(tokens // lanes):
            at = slice(block * lanes, (block + 1) * lanes)
            across = jnp.broadcast_to(scales[slot:slot + 1, at], (lanes, lanes)).T
            for col in range(width // lanes):
                cols = slice(col * lanes, (col + 1) * lanes)
                hbuf[0, slot, at, cols] = (codes[slot, at, cols].astype(F32) * across).astype(BF16)
    loads[1].wait()
    each(0, CHAINS, first_product)
    loads[2].wait()
    loads[3].wait()
    each(0, CHAINS, add_weight_grad)
    pl.semaphore_wait(barrier, len(greeted))

    each(0, CHAINS, scatter)

    @pl.when(is_top)
    def _():
        loads[4].wait()
        for tick in range(1, ticks + 1):
            hbuf[tick, 1] = loss_in[entry[tick - 1]]

    def top_ahead(step, do):
        tick, slot, half, row = where_of(step)

        @pl.when(jnp.logical_and(enters(slot), tick + 1 < ticks))
        def _():
            do(tick + 1, slot, half, row, first_top + 2 * tick + half)

    def top_start(step):
        top_ahead(step, lambda tick, slot, half, row, job: own_partial(tick, slot, row, job))

    def top_exchange(step):
        top_ahead(step, lambda tick, slot, half, row, job: own_exchange(tick, slot, half, job))

    def look_first(step):
        tick, slot, half, row = where_of(step)

        @pl.when(goes_down(slot))
        def _():
            part[first_q + step] = lax.dot_general(
                passed[step], down_in[slot], NT, preferred_element_type=F32).astype(BF16)
            scatter(first_q + step)

    def pass_first(step):
        tick, slot, half, row = where_of(step)

        @pl.when(goes_down(slot))
        def _():
            gsum[first_q + step] = gathered(first_q + step).astype(BF16)
            send_sum(step)

    def take(step):
        tick, slot, half, row = where_of(step)
        arrive(tick, slot, half, row)
        look_ahead(step)
        top_start(step)

    each(0, CHAINS, exchange_own)

    @pl.when(is_top)
    def _():
        down_copy(0, 1).start()

    @pl.when(jnp.logical_not(is_top))
    def _():
        down_copy(1, 1).start()

    @pl.when(jnp.logical_not(is_top))
    def _():
        down_copy(0, 0).start()

    each(0, CHAINS, finish_hidden)

    each(0, CHAINS, update)
    down_wait(1)
    each(0, 2, look_first)
    each(0, 2, top_start)
    cross_scatter(1)
    each(0, 2, pass_first)
    each(0, 2, top_exchange)
    cross_gather(1)
    take(CHAINS)
    down_wait(0)
    each(2, CHAINS, look_first)
    cross_scatter(0)
    each(2, CHAINS, pass_first)
    cross_gather(0)

    def main(step):
        @pl.when(jnp.logical_and(step > CHAINS, step < steps))
        def _():
            take(step)

        @pl.when(step < steps)
        def _():
            finish_hidden(step)

        @pl.when(step > CHAINS)
        def _():
            pass_sum(step - 1)
            top_exchange(step - 1)
            update(step - 1)

        @pl.when(step < steps)
        def _():
            add_weight_grad(step)

    each(CHAINS, steps + 1, main)

    def hand_out(chain):
        tick, slot, half, row = where_of(chain)
        arrive(ticks, slot, half, row)
        held_out[slot, pl.ds(row, rows), :] = hbuf[ticks, slot, pl.ds(row, rows), :]

    each(0, CHAINS, hand_out)

    def drain(step):
        tick, slot, half, row = where_of(step)
        wait_bytes(rs_in.at[0], ag_send.at[step])

        @pl.when(goes_down(slot))
        def _():
            wait_bytes(passed.at[step], h_send.at[step])

        @pl.when(jnp.logical_and(step < jobs_q, goes_down(slot)))
        def _():
            wait_bytes(rs_in.at[0], rs_send.at[first_q + step])
            wait_bytes(msg.at[0, 0, 0], msg_send.at[first_q + step])

    def drain_own(job):
        wait_bytes(rs_in.at[0], rs_send.at[job])
        wait_bytes(gsum.at[0], msg_send.at[job])

    def drain_cross(job):
        @pl.when(goes_down(lax.div(job, 2)))
        def _():
            wait_bytes(rs_in.at[0], rs_send.at[first_g + job])
            wait_bytes(rs_in.at[0], g_send.at[job])

    each(0, steps, drain)
    each(0, CHAINS, drain_own)
    each(0, CHAINS, drain_cross)
    wait_bytes(w_down.at[0], down_send.at[0])

    @pl.when(is_top)
    def _():
        each(first_top, first_top + 2 * (ticks - 1), drain_own)

    @pl.when(jnp.logical_not(is_top))
    def _():
        wait_bytes(w_down.at[1], down_send.at[1])


def solution(mesh):
    sections, tensors = mesh.shape["section"], mesh.shape["tensor"]
    group = tensors // 2

    def per_device(grad_codes, token_scales, loss_grads, entry_order, w_up, w_down, pre_act):
        slots, tokens, width = grad_codes.shape
        ticks, hid = pre_act.shape[1], pre_act.shape[3]
        rows = tokens // 2
        piece = rows // group
        steps = ticks * CHAINS
        jobs = CHAINS * (ticks + 1) + 2 * (ticks - 1)
        vmem = pl.BlockSpec(memory_space=pltpu.VMEM)
        hbm = pl.BlockSpec(memory_space=pl.ANY)
        dma = pltpu.SemaphoreType.DMA
        return pl.pallas_call(
            lambda *refs: relay_kernel((sections, group, ticks, tokens, width), *refs),
            out_shape=(pltpu.VMEM((slots, tokens, width), BF16), pltpu.VMEM((slots, hid, width), BF16)),
            in_specs=[vmem, pl.BlockSpec(memory_space=pltpu.SMEM), hbm, hbm, hbm, hbm, hbm],
            out_specs=(vmem, vmem),
            scratch_shapes=[
                pltpu.VMEM((slots, tokens, width), jnp.int32),
                pltpu.VMEM((slots, width, hid), BF16),
                pltpu.VMEM((slots, hid, width), BF16),
                pltpu.VMEM((slots, ticks, tokens, hid), BF16),
                pltpu.VMEM((ticks, tokens, width), BF16),
                pltpu.VMEM((slots, hid, width), BF16),
                pltpu.VMEM((ticks + 1, slots, tokens, width), BF16),
                pltpu.VMEM((steps, rows, width), BF16),
                pltpu.VMEM((jobs, rows, hid), BF16),
                pltpu.VMEM((jobs, group - 1, piece, hid), BF16),
                pltpu.VMEM((jobs, piece, hid), BF16),
                pltpu.VMEM((ticks, slots, 2, 2, piece, hid), BF16),
                pltpu.VMEM((steps, rows, hid), BF16),
                pltpu.VMEM((slots, hid, hid), BF16),
                pltpu.VMEM((slots, hid, width), F32),
                dma((5,)), dma((jobs,)), dma((jobs,)), dma((jobs,)), dma((ticks, slots, 2)), dma((steps,)),
                dma((steps,)), dma((CHAINS,)), dma((CHAINS,)), dma((steps,)), dma((ticks, slots, 2)),
                dma((slots,)), dma((slots,)),
            ],
            compiler_params=pltpu.CompilerParams(
                collective_id=0, has_side_effects=True, vmem_limit_bytes=56 * 1024 * 1024),
            cost_estimate=pl.CostEstimate(flops=4 * 10**9, bytes_accessed=9 * 10**6, transcendentals=0),
        )(token_scales, entry_order, grad_codes, w_up, w_down, pre_act, loss_grads)

    placed = (
        P("section", None, "tensor"),
        P("section", None),
        P(None, None, "tensor"),
        P(),
        P("section", "tensor", None),
        P("section", None, "tensor"),
        P("section", None, None, None),
    )
    return jax.shard_map(
        per_device,
        mesh=mesh,
        in_specs=placed,
        out_specs=(P("section", None, "tensor"), P("section", None, "tensor")),
        check_vma=False,
    )
```

```python
import jax
import jax.numpy as jnp
from jax import lax
from jax.experimental import pallas as pl
from jax.experimental.pallas import tpu as pltpu
from jax.sharding import PartitionSpec as P

MESH = pl.DeviceIdType.MESH
F32 = jnp.float32
BF16 = jnp.bfloat16
CHAINS = 4
NT = (((1,), (1,)), ((), ()))
TN = (((0,), (0,)), ((), ()))


def relay_kernel(dims, scales, entry, codes_hbm, up_hbm, down_hbm, pre_hbm, loss_hbm, held_out, grad_out,
                 codes, w_up, w_down, pre_act, loss_in, down_in, hbuf, passed, part, rs_in, gsum, msg, masked,
                 cross, total, load_sem, rs_send, rs_recv, msg_send, msg_recv, ag_send, ag_recv,
                 g_send, g_recv, h_send, h_recv, down_send, down_recv):
    sections, group, ticks, tokens, width = dims
    rows = tokens // 2
    piece = rows // group
    first_q, first_g, first_top = CHAINS, CHAINS * ticks, CHAINS * (ticks + 1)
    jobs_q = CHAINS * (ticks - 1)
    steps = CHAINS * ticks
    sec = lax.axis_index("section")
    ten = lax.axis_index("tensor")
    x_at = lax.div(ten, 4)
    z_at = lax.rem(lax.div(ten, 2), 2)
    core_at = lax.rem(ten, 2)
    mine = x_at * 2 + core_at
    partner = x_at * 4 + (1 - z_at) * 2 + core_at
    sec_below = lax.rem(sec + sections - 1, sections)
    sec_above = lax.rem(sec + 1, sections)
    is_top = sec == sections - 1
    keeps = lax.div(sec + sections - 1, sections)
    own_rows = pl.ds(pl.multiple_of(mine * piece, piece), piece)

    def peer(rel):
        other = lax.rem(mine + rel, group)
        return other, (sec, lax.div(other, 2) * 4 + z_at * 2 + lax.rem(other, 2))

    def send(src, dst, ssem, rsem, device):
        return pltpu.make_async_remote_copy(
            src_ref=src, dst_ref=dst, send_sem=ssem, recv_sem=rsem, device_id=device, device_id_type=MESH)

    def wait_bytes(ref, sem):
        pltpu.make_async_copy(ref, ref, sem).wait()

    def down_copy(slot, slot_to):
        return send(w_down.at[slot], down_in.at[slot_to], down_send.at[slot], down_recv.at[slot_to], (sec_above, ten))

    def where_of(step):
        tick = lax.div(step, CHAINS)
        chain = lax.rem(step, CHAINS)
        half = lax.rem(chain, 2)
        return tick, 1 - lax.div(chain, 2), half, pl.multiple_of(half * rows, rows)

    def goes_down(slot):
        return sec + slot > 0

    def enters(slot):
        return sec + slot == sections

    def scatter(job):
        for rel in range(1, group):
            other, device = peer(rel)
            send(part.at[job, pl.ds(pl.multiple_of(other * piece, piece), piece)], rs_in.at[job, rel - 1],
                 rs_send.at[job], rs_recv.at[job], device).start()

    def gathered(job):
        wait_bytes(rs_in.at[job], rs_recv.at[job])
        acc = part[job, own_rows, :].astype(F32)
        for rel in range(1, group):
            acc = acc + rs_in[job, rel - 1].astype(F32)
        return acc

    def own_partial(tick, slot, row, job):
        part[job] = lax.dot_general(
            hbuf[tick, slot, pl.ds(row, rows), :], w_down[slot], NT, preferred_element_type=F32).astype(BF16)
        scatter(job)

    def own_exchange(tick, slot, half, job):
        gsum[job] = gathered(job).astype(BF16)
        msg[tick, slot, half, z_at] = gsum[job]
        send(gsum.at[job], msg.at[tick, slot, half, z_at], msg_send.at[job], msg_recv.at[tick, slot, half],
             (sec, partner)).start()

    def arrive(tick, slot, half, row):
        @pl.when(jnp.logical_not(enters(slot)))
        def _():
            wait_bytes(hbuf.at[tick, slot, pl.ds(row, rows)], h_recv.at[tick - 1, slot, half])

    def look_ahead(step):
        tick, slot, half, row = where_of(step)

        @pl.when(jnp.logical_and(step < jobs_q, goes_down(slot)))
        def _():
            job = first_q + step
            part[job] = lax.dot_general(
                hbuf[tick, slot, pl.ds(row, rows), :], down_in[slot], NT, preferred_element_type=F32).astype(BF16)
            scatter(job)

    def send_sum(step):
        tick, slot, half, row = where_of(step)
        for to in (ten, partner):
            send(gsum.at[first_q + step], msg.at[tick + 1, slot * keeps, half, z_at], msg_send.at[first_q + step],
                 msg_recv.at[tick + 1, slot * keeps, half], (sec_below, to)).start()

    def pass_sum(step):
        tick, slot, half, row = where_of(step)

        @pl.when(jnp.logical_and(step < jobs_q, goes_down(slot)))
        def _():
            @pl.when(jnp.logical_and(tick == 1, half == 0))
            def _():
                for part_of in range(2):
                    wait_bytes(rs_in.at[0], g_recv.at[slot * 2 + part_of])

            gsum[first_q + step] = (gathered(first_q + step) + jnp.dot(
                masked[step, own_rows, :], cross[slot], preferred_element_type=F32)).astype(BF16)
            send_sum(step)

    def finish_hidden(step):
        tick, slot, half, row = where_of(step)
        from_own = jnp.logical_or(tick == 0, enters(slot))

        @pl.when(from_own)
        def _():
            wait_bytes(gsum.at[0], msg_recv.at[tick, slot, half])

        @pl.when(jnp.logical_not(from_own))
        def _():
            wait_bytes(msg.at[tick, slot, half], msg_recv.at[tick, slot, half])

        hidden = msg[tick, slot, half, 0].astype(F32) + msg[tick, slot, half, 1].astype(F32)
        pre = pre_act[slot, tick, pl.ds(pl.multiple_of(row + mine * piece, piece), piece), :]
        masked[step, own_rows, :] = jnp.where(pre.astype(F32) > 0, hidden, 0.0).astype(BF16)
        for rel in range(1, group):
            send(masked.at[step, own_rows], masked.at[step, own_rows], ag_send.at[step], ag_recv.at[step],
                 peer(rel)[1]).start()

    def update(step):
        tick, slot, half, row = where_of(step)
        wait_bytes(rs_in.at[0], ag_recv.at[step])

        @pl.when(goes_down(slot))
        def _():
            branch = lax.dot_general(masked[step], w_up[slot], NT, preferred_element_type=F32)
            passed[step] = (hbuf[tick, slot, pl.ds(row, rows), :].astype(F32) + branch).astype(BF16)
            send(passed.at[step], hbuf.at[tick + 1, slot * keeps, pl.ds(row, rows)], h_send.at[step],
                 h_recv.at[tick, slot * keeps, half], (sec_below, ten)).start()

    def add_weight_grad(step):
        tick, slot, half, row = where_of(step)

        @pl.when(half == 1)
        def _():
            active = jnp.maximum(pre_act[slot, tick], 0)
            total[slot] += lax.dot_general(active, hbuf[tick, slot], TN, preferred_element_type=F32)

        @pl.when(jnp.logical_and(half == 1, tick == ticks - 1))
        def _():
            grad_out[slot] = total[slot].astype(BF16)

    def down_wait(slot):
        @pl.when(goes_down(slot))
        def _():
            wait_bytes(down_in.at[slot], down_recv.at[slot])

    def cross_scatter(slot):
        @pl.when(goes_down(slot))
        def _():
            term = lax.dot_general(w_up[slot], down_in[slot], (((0,), (1,)), ((), ())), preferred_element_type=F32)
            for half in range(2):
                part[first_g + slot * 2 + half] = term[half * rows:(half + 1) * rows].astype(BF16)
                scatter(first_g + slot * 2 + half)

    def cross_gather(slot):
        @pl.when(goes_down(slot))
        def _():
            for half in range(2):
                job = first_g + slot * 2 + half
                at = pl.ds(pl.multiple_of(half * rows + mine * piece, piece), piece)
                cross[slot, at, :] = gathered(job).astype(BF16)
                for rel in range(1, group):
                    send(cross.at[slot, at], cross.at[slot, at], g_send.at[slot * 2 + half],
                         g_recv.at[slot * 2 + half], peer(rel)[1]).start()

    def each(first, last, do):
        def body(step, carry):
            do(step)
            return carry

        lax.fori_loop(first, last, body, 0)

    def exchange_own(step):
        tick, slot, half, row = where_of(step)
        own_exchange(0, slot, half, step)

    def first_product(step):
        tick, slot, half, row = where_of(step)
        part[step] = lax.dot_general(
            hbuf[0, slot, pl.ds(row, rows), :], w_down[slot], NT, preferred_element_type=F32).astype(BF16)

    barrier = pltpu.get_barrier_semaphore()
    greeted = [(sec_below, partner), (sec_above, partner), (sec, partner), (sec_below, ten), (sec_above, ten)]
    greeted += [peer(rel)[1] for rel in range(1, group)]
    for other in greeted:
        pl.semaphore_signal(barrier, inc=1, device_id=other, device_id_type=MESH)

    loads = [pltpu.make_async_copy(src, dst, load_sem.at[i]) for i, (src, dst) in enumerate((
        (codes_hbm, codes), (down_hbm, w_down), (up_hbm, w_up), (pre_hbm, pre_act), (loss_hbm, loss_in)))]
    for load in loads[:4]:
        load.start()

    @pl.when(is_top)
    def _():
        loads[4].start()

    total[...] = jnp.zeros_like(total)
    loads[0].wait()
    lanes = min(128, rows)
    for slot in range(2):
        for block in range(tokens // lanes):
            at = slice(block * lanes, (block + 1) * lanes)
            across = jnp.broadcast_to(scales[slot:slot + 1, at], (lanes, lanes)).T
            for col in range(width // lanes):
                cols = slice(col * lanes, (col + 1) * lanes)
                hbuf[0, slot, at, cols] = (codes[slot, at, cols].astype(F32) * across).astype(BF16)
    loads[1].wait()
    each(0, CHAINS, first_product)
    loads[2].wait()
    loads[3].wait()
    each(0, CHAINS, add_weight_grad)
    pl.semaphore_wait(barrier, len(greeted))

    each(0, CHAINS, scatter)

    @pl.when(is_top)
    def _():
        loads[4].wait()
        for tick in range(1, ticks + 1):
            hbuf[tick, 1] = loss_in[entry[tick - 1]]

    def top_ahead(step, do):
        tick, slot, half, row = where_of(step)

        @pl.when(jnp.logical_and(enters(slot), tick + 1 < ticks))
        def _():
            do(tick + 1, slot, half, row, first_top + 2 * tick + half)

    def top_start(step):
        top_ahead(step, lambda tick, slot, half, row, job: own_partial(tick, slot, row, job))

    def top_exchange(step):
        top_ahead(step, lambda tick, slot, half, row, job: own_exchange(tick, slot, half, job))

    def look_first(step):
        tick, slot, half, row = where_of(step)

        @pl.when(goes_down(slot))
        def _():
            part[first_q + step] = lax.dot_general(
                passed[step], down_in[slot], NT, preferred_element_type=F32).astype(BF16)
            scatter(first_q + step)

    def pass_first(step):
        tick, slot, half, row = where_of(step)

        @pl.when(goes_down(slot))
        def _():
            gsum[first_q + step] = gathered(first_q + step).astype(BF16)
            send_sum(step)

    def take(step):
        tick, slot, half, row = where_of(step)
        arrive(tick, slot, half, row)
        look_ahead(step)
        top_start(step)

    each(0, CHAINS, exchange_own)

    @pl.when(is_top)
    def _():
        down_copy(0, 1).start()

    @pl.when(jnp.logical_not(is_top))
    def _():
        down_copy(1, 1).start()

    each(0, CHAINS, finish_hidden)

    @pl.when(jnp.logical_not(is_top))
    def _():
        down_copy(0, 0).start()


    each(0, 2, update)
    down_wait(1)
    each(0, 2, look_first)
    each(0, 2, top_start)
    cross_scatter(1)
    each(0, 2, pass_first)
    each(0, 2, top_exchange)
    each(2, CHAINS, update)
    cross_gather(1)
    down_wait(0)
    each(2, CHAINS, look_first)
    cross_scatter(0)
    take(CHAINS)
    each(2, CHAINS, pass_first)
    cross_gather(0)

    def main(step):
        @pl.when(jnp.logical_and(step > CHAINS, step < steps))
        def _():
            take(step)

        @pl.when(step < steps)
        def _():
            finish_hidden(step)

        @pl.when(step > CHAINS)
        def _():
            pass_sum(step - 1)
            top_exchange(step - 1)
            update(step - 1)
            add_weight_grad(step - 1)

    each(CHAINS, steps + 1, main)

    def hand_out(chain):
        tick, slot, half, row = where_of(chain)
        arrive(ticks, slot, half, row)
        held_out[slot, pl.ds(row, rows), :] = hbuf[ticks, slot, pl.ds(row, rows), :]

    each(0, CHAINS, hand_out)

    def drain(step):
        tick, slot, half, row = where_of(step)
        wait_bytes(rs_in.at[0], ag_send.at[step])

        @pl.when(goes_down(slot))
        def _():
            wait_bytes(passed.at[step], h_send.at[step])

        @pl.when(jnp.logical_and(step < jobs_q, goes_down(slot)))
        def _():
            wait_bytes(rs_in.at[0], rs_send.at[first_q + step])
            wait_bytes(msg.at[0, 0, 0], msg_send.at[first_q + step])

    def drain_own(job):
        wait_bytes(rs_in.at[0], rs_send.at[job])
        wait_bytes(gsum.at[0], msg_send.at[job])

    def drain_cross(job):
        @pl.when(goes_down(lax.div(job, 2)))
        def _():
            wait_bytes(rs_in.at[0], rs_send.at[first_g + job])
            wait_bytes(rs_in.at[0], g_send.at[job])

    each(0, steps, drain)
    each(0, CHAINS, drain_own)
    each(0, CHAINS, drain_cross)
    wait_bytes(w_down.at[0], down_send.at[0])

    @pl.when(is_top)
    def _():
        each(first_top, first_top + 2 * (ticks - 1), drain_own)

    @pl.when(jnp.logical_not(is_top))
    def _():
        wait_bytes(w_down.at[1], down_send.at[1])


def solution(mesh):
    sections, tensors = mesh.shape["section"], mesh.shape["tensor"]
    group = tensors // 2

    def per_device(grad_codes, token_scales, loss_grads, entry_order, w_up, w_down, pre_act):
        slots, tokens, width = grad_codes.shape
        ticks, hid = pre_act.shape[1], pre_act.shape[3]
        rows = tokens // 2
        piece = rows // group
        steps = ticks * CHAINS
        jobs = CHAINS * (ticks + 1) + 2 * (ticks - 1)
        vmem = pl.BlockSpec(memory_space=pltpu.VMEM)
        hbm = pl.BlockSpec(memory_space=pl.ANY)
        dma = pltpu.SemaphoreType.DMA
        return pl.pallas_call(
            lambda *refs: relay_kernel((sections, group, ticks, tokens, width), *refs),
            out_shape=(pltpu.VMEM((slots, tokens, width), BF16), pltpu.VMEM((slots, hid, width), BF16)),
            in_specs=[vmem, pl.BlockSpec(memory_space=pltpu.SMEM), hbm, hbm, hbm, hbm, hbm],
            out_specs=(vmem, vmem),
            scratch_shapes=[
                pltpu.VMEM((slots, tokens, width), jnp.int32),
                pltpu.VMEM((slots, width, hid), BF16),
                pltpu.VMEM((slots, hid, width), BF16),
                pltpu.VMEM((slots, ticks, tokens, hid), BF16),
                pltpu.VMEM((ticks, tokens, width), BF16),
                pltpu.VMEM((slots, hid, width), BF16),
                pltpu.VMEM((ticks + 1, slots, tokens, width), BF16),
                pltpu.VMEM((steps, rows, width), BF16),
                pltpu.VMEM((jobs, rows, hid), BF16),
                pltpu.VMEM((jobs, group - 1, piece, hid), BF16),
                pltpu.VMEM((jobs, piece, hid), BF16),
                pltpu.VMEM((ticks, slots, 2, 2, piece, hid), BF16),
                pltpu.VMEM((steps, rows, hid), BF16),
                pltpu.VMEM((slots, hid, hid), BF16),
                pltpu.VMEM((slots, hid, width), F32),
                dma((5,)), dma((jobs,)), dma((jobs,)), dma((jobs,)), dma((ticks, slots, 2)), dma((steps,)),
                dma((steps,)), dma((CHAINS,)), dma((CHAINS,)), dma((steps,)), dma((ticks, slots, 2)),
                dma((slots,)), dma((slots,)),
            ],
            compiler_params=pltpu.CompilerParams(
                collective_id=0, has_side_effects=True, vmem_limit_bytes=56 * 1024 * 1024),
            cost_estimate=pl.CostEstimate(flops=4 * 10**9, bytes_accessed=9 * 10**6, transcendentals=0),
        )(token_scales, entry_order, grad_codes, w_up, w_down, pre_act, loss_grads)

    placed = (
        P("section", None, "tensor"),
        P("section", None),
        P(None, None, "tensor"),
        P(),
        P("section", "tensor", None),
        P("section", None, "tensor"),
        P("section", None, None, None),
    )
    return jax.shard_map(
        per_device,
        mesh=mesh,
        in_specs=placed,
        out_specs=(P("section", None, "tensor"), P("section", None, "tensor")),
        check_vma=False,
    )
```
